32 devices in a mesh: groups: 2 (over y), ctx: 4 (over z), head: 2 (over x), section: 2 (over core).
Axes of the slice: x: 2, y: 2, z: 4, core: 2. Of those that a mesh axis runs over, the one named last changes fastest.
Arguments:
- queries_in: bfloat16 [2, 2048, 1024], P('section', ('groups', 'ctx'), 'head'), parts along dimension 1, may hold values from -6 to 6
- keys_in: bfloat16 [2, 2048, 1024], P('section', ('groups', 'ctx'), 'head'), parts along dimension 1, may hold values from -6 to 6
- values_in: bfloat16 [2048, 2048], P(('groups', 'ctx'), 'head'), parts along dimension 0, may hold values from -6 to 6
- gate_in: bfloat16 [2, 2048, 2048], P('section', ('groups', 'ctx'), 'head'), parts along dimension 1, may hold values from -6 to 6
- decay_in: float32 [2, 2048, 16], P('section', ('groups', 'ctx'), 'head'), parts along dimension 1, may hold values from -3 to 3072
- write_in: float32 [2, 2048, 16], P('section', ('groups', 'ctx'), 'head'), parts along dimension 1, may hold values from -16 to 2
- decay_log: float32 [2, 16], P('section', 'head'), may hold values from -16 to -2
- conv_query: bfloat16 [2, 4, 1024], P('section', None, 'head'), may hold values from -3 to 3
- conv_key: bfloat16 [2, 4, 1024], P('section', None, 'head'), may hold values from -3 to 3
- conv_value: bfloat16 [2, 4, 2048], P('section', None, 'head'), may hold values from -3 to 3
- norm_gain: float32 [2, 128], P('section'), may hold values from 0.25 to 1.75
- segment_ids: int32 [2048], P(('groups', 'ctx')), parts along dimension 0, may hold values from 0 to 3, never falling along the last dimension, each value on 1 to 512 neighbouring positions
Outputs:
- layer_out: bfloat16 [2, 2048, 2048], P('section', ('groups', 'ctx'), 'head'), parts along dimension 1
The draws below stay inside these ranges and needn't reach their ends.
There are 2 independent parts, one for each index of `groups`. The reference program is written for one: setup_inputs(seed, part) draws one part's arguments, and reference() takes and returns one part's arrays. A program takes and returns all parts, laid end to end along the dimension named above; an argument that names none is the same for every part. Nothing has to cross between parts.
All inputs are finite; a program needn't handle non-finite values.
Results may differ from the reference program's by a relative error of at most 0.0033.
Values may be sent and summed in bfloat16 or wider, within the bound.
A program may use at most 128 MiB of HBM per device.

```python
import math
import jax
import jax.numpy as jnp
import numpy as np
from jax import lax

DK = 128
DV = 128
VALUE_HEADS = 16
HK = 8
CONV = 4
SEGS = 4
TOK_DEV = 256
TOKEN_COUNT = 1024
LAYER_COUNT = 2


def draw_decay_in(key, part):
    random_key_split = jax.random.split(key, 4)
    baseline_output = jnp.clip(jax.random.normal(random_key_split[0], (LAYER_COUNT, TOKEN_COUNT, VALUE_HEADS), jnp.float32), -1.5, 1.5)
    block_offset = jax.random.uniform(random_key_split[1], (LAYER_COUNT, TOKEN_COUNT // TOK_DEV, 1, VALUE_HEADS), jnp.float32, -0.7, 0.7)
    block_offset = jnp.broadcast_to(block_offset, (LAYER_COUNT, TOKEN_COUNT // TOK_DEV, TOK_DEV, VALUE_HEADS)).reshape(LAYER_COUNT, TOKEN_COUNT, VALUE_HEADS)
    spike_positions = jax.random.randint(random_key_split[2], (LAYER_COUNT, 2, 1), 0, TOKEN_COUNT)
    token_positions = jnp.arange(TOKEN_COUNT)[None, None, :]
    spike_mask = jnp.any(token_positions == spike_positions, axis=1)
    spike_length = TOKEN_COUNT * jax.random.uniform(random_key_split[3], (LAYER_COUNT, TOKEN_COUNT, VALUE_HEADS), jnp.float32, 2.0, 3.0)
    return jnp.where(spike_mask[:, :, None], spike_length, baseline_output + block_offset)


def draw_decay_log(key, part):
    random_key_split = jax.random.split(key, 3)
    share = 0.3
    chance = jax.random.uniform(random_key_split[0], (LAYER_COUNT, VALUE_HEADS), jnp.float32)
    slow_log = jax.random.uniform(random_key_split[1], (LAYER_COUNT, VALUE_HEADS), jnp.float32, math.log(0.1), math.log(0.25)) - math.log(TOKEN_COUNT)
    fast_log = jax.random.uniform(random_key_split[2], (LAYER_COUNT, VALUE_HEADS), jnp.float32, math.log(0.02), math.log(0.05))
    return jnp.where(chance < share, fast_log, slow_log)


def draw_write_in(key, part):
    random_key_split = jax.random.split(key, 3)
    share = 0.35
    chance = jax.random.uniform(random_key_split[0], (LAYER_COUNT, 1, VALUE_HEADS), jnp.float32)
    strong = jax.random.uniform(random_key_split[1], (LAYER_COUNT, TOKEN_COUNT, VALUE_HEADS), jnp.float32, 0.2, 0.8)
    weak = DK / TOKEN_COUNT * jnp.exp(jax.random.uniform(random_key_split[2], (LAYER_COUNT, TOKEN_COUNT, VALUE_HEADS), jnp.float32, math.log(0.15), math.log(0.6)))
    strength = jnp.where(chance < share, strong, weak)
    return jnp.log(strength) - jnp.log1p(-strength)


def block_levels(stream_key, extent, cuts, low, high):
    level = 1.0
    for dim, blocks in cuts:
        heights = jax.random.uniform(jax.random.fold_in(jax.random.fold_in(stream_key, 6), dim), (blocks,), jnp.float32, low / len(cuts), high / len(cuts))
        level = level * jnp.repeat(jnp.exp(heights), extent[dim] // blocks).reshape((-1,) + (1,) * (len(extent) - 1 - dim))
    return level


def split_up(count, total, most, lean):
    loads = [(1 << 20) // math.isqrt(rank ** lean) + 1 for rank in range(2, count + 1)]
    surplus, given = total - most - (count - 1), [1] * (count - 1)
    while surplus > 0:
        free = [i for i in range(count - 1) if given[i] < most]
        whole, remaining = sum([loads[i] for i in free]), surplus
        for i in free:
            addition = min(most - given[i], max(1, remaining * loads[i] // whole), surplus)
            given[i] = given[i] + addition
            surplus = surplus - addition
    return np.array([most] + given)


def uneven(stream_key, number_of, total, reach, skew):
    if number_of == 2:
        one = jax.random.randint(stream_key, (), max(1, total - reach), min(reach, total - 1) + 1)
        return jnp.stack([one, total - one])
    tallies = jnp.asarray(split_up(number_of, total, reach, skew), jnp.int32)
    pairs = (number_of - 1) // 2
    source_of, taker = tallies[1:1 + 2 * pairs:2], tallies[2:2 + 2 * pairs:2]
    slack = jnp.minimum(source_of - 1, reach - taker)
    moved = jax.random.randint(jax.random.fold_in(stream_key, 1), (pairs,), 0, 1 << 20) % (slack + 1)
    tallies = tallies.at[1:1 + 2 * pairs:2].set(source_of - moved).at[2:2 + 2 * pairs:2].set(taker + moved)
    return tallies[jax.random.permutation(jax.random.fold_in(stream_key, 2), number_of)]


def scatter_about(key, extent, width, reach, shards=(), kind=jnp.bfloat16):
    level = block_levels(key, extent, shards, -0.22, 0.18) if shards else 1.0
    array = jax.random.normal(key, extent, jnp.float32) * width * level
    return jnp.minimum(jnp.maximum(array, -reach), reach).astype(kind)


def setup_inputs(seed: int = 0, part: int = 0) -> dict:
    key_list = jax.random.split(jax.random.key(seed), 13)
    part_keys = jax.random.split(jax.random.fold_in(key_list[12], part), 13)
    queries_in = scatter_about(part_keys[0], (LAYER_COUNT, TOKEN_COUNT, HK * DK), 1.0, 6.0, ((0, 2), (1, 4), (2, 2)))
    keys_in = scatter_about(part_keys[1], (LAYER_COUNT, TOKEN_COUNT, HK * DK), 1.0, 6.0, ((0, 2), (1, 4), (2, 2)))
    values_in = scatter_about(part_keys[2], (TOKEN_COUNT, VALUE_HEADS * DV), 1.0, 6.0, ((0, 4), (1, 2)))
    gate_in = scatter_about(part_keys[3], (LAYER_COUNT, TOKEN_COUNT, VALUE_HEADS * DV), 1.0, 6.0, ((0, 2), (1, 4), (2, 2)))
    decay_in = draw_decay_in(jax.random.fold_in(jax.random.fold_in(key_list[12], part), 71), part)
    write_in = draw_write_in(jax.random.fold_in(jax.random.fold_in(key_list[12], part), 71), part)
    decay_log = draw_decay_log(jax.random.fold_in(key_list[12], 71), part)
    conv_query = scatter_about(key_list[7], (LAYER_COUNT, CONV, HK * DK), CONV ** -0.5, 3.0, ((0, 2), (2, 2)))
    conv_key = scatter_about(key_list[8], (LAYER_COUNT, CONV, HK * DK), CONV ** -0.5, 3.0, ((0, 2), (2, 2)))
    conv_value = scatter_about(key_list[9], (LAYER_COUNT, CONV, VALUE_HEADS * DV), CONV ** -0.5, 3.0, ((0, 2), (2, 2)))
    norm_gain = jnp.clip(1.0 + 0.15 * jax.random.normal(key_list[10], (LAYER_COUNT, DV), jnp.float32), 0.25, 1.75)
    segment_ids = jnp.searchsorted(jnp.cumsum(uneven(part_keys[11], SEGS, TOKEN_COUNT, TOKEN_COUNT // 2, 0)), jnp.arange(TOKEN_COUNT), side="right").astype(jnp.int32)
    return {"queries_in": queries_in, "keys_in": keys_in, "values_in": values_in, "gate_in": gate_in, "decay_in": decay_in, "write_in": write_in, "decay_log": decay_log, "conv_query": conv_query, "conv_key": conv_key, "conv_value": conv_value, "norm_gain": norm_gain, "segment_ids": segment_ids}


highest_precision = lax.Precision.HIGHEST

def causal_conv(inputs, weight, segment_ids):
    length = inputs.shape[0]
    taps = weight.shape[0]
    summed = jnp.zeros_like(inputs)
    for offset in range(taps):
        moved = jnp.concatenate([jnp.zeros((offset, inputs.shape[1]), inputs.dtype), inputs[:length - offset]], axis=0)
        moved_seg = jnp.concatenate([jnp.full((offset,), -1, jnp.int32), segment_ids[:length - offset]], axis=0)
        keeping = (moved_seg == segment_ids)[:, None]
        summed = summed + jnp.where(keeping, moved, 0.0) * weight[taps - 1 - offset].astype(inputs.dtype)[None, :]
    return jax.nn.silu(summed)

def unit_rows(values):
    return values * lax.rsqrt(lax.optimization_barrier(jnp.sum(values * values, axis=-1, keepdims=True)) + 1e-06)

def mixer(query_raw, key_raw, value_raw, gate_raw, decay_raw, write_raw, rate_log, taps_query, taps_key, taps_value, gain, segment_ids):
    ftype = jnp.float32
    queries = unit_rows(causal_conv(query_raw.astype(ftype), taps_query, segment_ids).reshape(TOKEN_COUNT, HK, DK))
    keys = unit_rows(causal_conv(key_raw.astype(ftype), taps_key, segment_ids).reshape(TOKEN_COUNT, HK, DK))
    values = causal_conv(value_raw.astype(ftype), taps_value, segment_ids).reshape(TOKEN_COUNT, VALUE_HEADS, DV)
    queries = jnp.repeat(queries, VALUE_HEADS // HK, axis=1)
    keys = jnp.repeat(keys, VALUE_HEADS // HK, axis=1)
    log_decay = -jnp.exp(rate_log)[None, :] * jax.nn.softplus(decay_raw)
    previous = jnp.concatenate([segment_ids[:1], segment_ids[:-1]])
    rates = jnp.where((segment_ids == previous)[:, None], jnp.exp(log_decay), 0.0)
    betas = jax.nn.sigmoid(write_raw)

    def advance(memory_state, inputs):
        single_query, single_key, value_row, rate_row, beta_row = inputs
        retained_state = rate_row[:, None, None] * memory_state
        retrieved_values = jnp.einsum('zp,zpd->zd', single_key, retained_state, precision=highest_precision)
        update = beta_row[:, None] * (value_row - retrieved_values)
        memory_state = retained_state + single_key[:, :, None] * update[:, None, :]
        mixer_result = jnp.einsum('zp,zpd->zd', single_query, memory_state, precision=highest_precision)
        return (memory_state, mixer_result)
    start_state = jnp.zeros((VALUE_HEADS, DK, DV), ftype)
    _, mixed = lax.scan(advance, start_state, (queries, keys, values, rates, betas))
    norm_scale = lax.rsqrt(lax.optimization_barrier(jnp.mean(mixed * mixed, axis=-1, keepdims=True)) + 1e-06)
    gate_act = jax.nn.silu(gate_raw.astype(ftype)).reshape(TOKEN_COUNT, VALUE_HEADS, DV)
    output = mixed * norm_scale * gain[None, None, :] * gate_act
    return output.reshape(TOKEN_COUNT, VALUE_HEADS * DV).astype(jnp.bfloat16)

def reference(queries_in, keys_in, values_in, gate_in, decay_in, write_in, decay_log, conv_query, conv_key, conv_value, norm_gain, segment_ids):
    layer_values = values_in
    results = []
    for layer_index in range(LAYER_COUNT):
        produced = mixer(queries_in[layer_index], keys_in[layer_index], layer_values, gate_in[layer_index], decay_in[layer_index], write_in[layer_index], decay_log[layer_index], conv_query[layer_index], conv_key[layer_index], conv_value[layer_index], norm_gain[layer_index], segment_ids)
        results.append(produced)
        layer_values = produced
    return jnp.stack(results)
```

```python
import functools

import jax
import jax.numpy as jnp
from jax import lax
from jax.experimental import pallas as pl
from jax.experimental.pallas import tpu as pltpu
from jax.sharding import PartitionSpec as P

D = 128
RIM = 16
CONV = 4
SIZES = (1, 2, 4, 8, 16, 32, 64)
bf16 = jnp.bfloat16
f32 = jnp.float32
MESH = pl.DeviceIdType.MESH


def split(x):
    high = x.astype(bf16)
    return high, (x - high.astype(f32)).astype(bf16)


def dot(a, b):
    return jnp.dot(a, b, preferred_element_type=f32)


def dot_nt(a, b):
    return lax.dot_general(a, b, (((1,), (1,)), ((), ())), preferred_element_type=f32)


def mm(a, b, one=dot):
    return one(a[0], b[0]) + (one(a[0], b[1]) + one(a[1], b[0]))


def sigmoid(x):
    return 1.0 / (1.0 + jnp.exp(-x))


def iota(shape, dim):
    return lax.broadcasted_iota(jnp.int32, shape, dim)


def inverses(parts, mask):
    eye = (iota((D, D), 0) == iota((D, D), 1)).astype(f32)
    inv = [eye - a * mask[0] for a in parts]
    for i in range(1, len(SIZES)):
        halves = [split(t) for t in inv]
        lower = [split(a * mask[i]) for a in parts]
        mid = [split(mm(t, a)) for t, a in zip(halves, lower)]
        inv = [t - mm(m, h) for t, m, h in zip(inv, mid, halves)]
    return inv


def kernel(
    nctx, q_in, k_in, v_in, g_in, dw_in, small_in, seg_in, out,
    qbuf, kbuf, vbuf, gbuf, dw, small, seg, segp, o1,
    xs, segx, keep, pair, dmask, cum, cumt, beta, betat,
    zh, zl, yh, yl, bv, s_in, s_out,
    loc_sem, x_send, x_recv, r_send, r_recv, c_send, c_recv, o_send, o_recv, o_loc, v_send, v_recv,
):
    T = q_in.shape[1]
    HQ = q_in.shape[2] // 2
    HV = v_in.shape[1] // 2
    NH = HV // D
    NK = HQ // D
    REP = NH // NK
    s = lax.axis_index("section")
    o = 1 - s
    c = lax.axis_index("ctx")
    has_prev = c > 0
    has_next = c < nctx - 1

    def cols(half, width):
        return pl.ds(pl.multiple_of(half * width, width), width)

    body = pl.ds(RIM, T)
    tail = pl.ds(T - RIM, RIM)
    rim = pl.ds(0, RIM)

    local = [
        (q_in.at[0, :, cols(s, HQ)], qbuf.at[s, body]),
        (k_in.at[0, :, cols(s, HQ)], kbuf.at[s, body]),
        (g_in.at[0, :, cols(s, HV)], gbuf.at[s]),
        (v_in.at[:, cols(s, HV)], vbuf.at[0, body]),
        (dw_in, dw.at[s]),
        (small_in, small.at[s]),
        (seg_in, seg),
    ]
    local = [pltpu.make_async_copy(a, b, loc_sem.at[i]) for i, (a, b) in enumerate(local)]
    for cp in local:
        cp.start()

    barrier = pltpu.get_barrier_semaphore()
    pl.semaphore_signal(barrier, inc=1, device_id={"section": o}, device_id_type=MESH)
    for ok, other in ((has_prev, c - 1), (has_next, c + 1)):

        @pl.when(ok)
        def _():
            for sec in (s, o):
                pl.semaphore_signal(
                    barrier, inc=1, device_id={"ctx": other, "section": sec}, device_id_type=MESH
                )

    pl.semaphore_wait(
        barrier, 1 + 2 * has_prev.astype(jnp.int32) + 2 * has_next.astype(jnp.int32)
    )

    def remote(src, dst, send, recv, where):
        return pltpu.make_async_remote_copy(
            src_ref=src, dst_ref=dst, send_sem=send, recv_sem=recv,
            device_id=where, device_id_type=MESH,
        )

    partner = {"section": o}
    ahead = {"ctx": c + 1}
    ahead_o = {"ctx": c + 1, "section": o}
    swaps = [
        (dw_in, dw.at[s]),
        (small_in, small.at[s]),
        (k_in.at[0, :, cols(o, HQ)], kbuf.at[s, body]),
        (q_in.at[0, :, cols(o, HQ)], qbuf.at[s, body]),
        (g_in.at[0, :, cols(o, HV)], gbuf.at[s]),
    ]
    swaps = [
        remote(a, b, x_send.at[i], x_recv.at[i], partner) for i, (a, b) in enumerate(swaps)
    ]
    rims = [
        (seg_in, segp, ahead),
        (k_in.at[0, tail, cols(s, HQ)], kbuf.at[s, rim], ahead),
        (q_in.at[0, tail, cols(s, HQ)], qbuf.at[s, rim], ahead),
        (k_in.at[0, tail, cols(o, HQ)], kbuf.at[s, rim], ahead_o),
        (q_in.at[0, tail, cols(o, HQ)], qbuf.at[s, rim], ahead_o),
        (v_in.at[tail, cols(s, HV)], vbuf.at[0, rim], ahead),
    ]
    rims = [
        remote(a, b, r_send.at[i], r_recv.at[i], w) for i, (a, b, w) in enumerate(rims)
    ]

    @pl.when(has_next)
    def _():
        for cp in rims:
            cp.start()

    for cp in swaps:
        cp.start()

    @pl.when(jnp.logical_not(has_prev))
    def _():
        segp[...] = jnp.zeros_like(segp)
        for layer in range(2):
            kbuf[layer, 0:RIM, :] = jnp.zeros((RIM, HQ), bf16)
            qbuf[layer, 0:RIM, :] = jnp.zeros((RIM, HQ), bf16)
            vbuf[layer, 0:RIM, :] = jnp.zeros((RIM, HV), bf16)
            for h in range(NH):
                s_in[layer, h] = jnp.zeros((D, D), f32)

    row = iota((D, D), 0)
    col = iota((D, D), 1)
    for i, size in enumerate(SIZES):
        down = row // size
        right = col // size
        dmask[i] = jnp.where((down == right + 1) & (down % 2 == 1), 1.0, 0.0)
    trow = iota((T, T), 0)
    tcol = iota((T, T), 1)

    for cp in local:
        cp.wait()
    for cp in swaps:
        cp.wait_recv()

    @pl.when(has_prev)
    def _():
        for cp in rims:
            cp.wait_recv()

    seg_row = seg[0:1, :].astype(f32)
    before = jnp.transpose(jnp.broadcast_to(segp[0:1, :].astype(f32), (D, T)))
    own = jnp.transpose(jnp.broadcast_to(seg_row, (D, T)))
    segx[0:RIM, :] = before[T - RIM :, :]
    segx[RIM:, :] = own
    for j in range(CONV - 1):
        keep[j] = jnp.where(segx[RIM - 3 + j : RIM - 3 + j + T, :] == own, 1.0, 0.0)
    last = before[T - 1 : T, :]
    keep[CONV - 1] = jnp.where(own == last, 1.0, 0.0)
    own_wide = jnp.concatenate([own] * (T // D), axis=1)
    pair[...] = jnp.where((own_wide == seg_row) & (trow >= tcol), 1.0, 0.0)

    lane = iota((T, D), 1)
    tri = jnp.where(trow >= tcol, 1.0, 0.0).astype(bf16)
    for layer in range(2):
        x = dw[layer]
        rate = small[layer, 5:6, 0:D]
        soft = jnp.maximum(x, 0.0) + jnp.log1p(jnp.exp(-jnp.abs(x)))
        decay = jnp.where(lane < 2 * NH, jnp.maximum(-jnp.exp(rate) * soft, -104.0), 0.0)
        p0 = decay.astype(bf16)
        rest = decay - p0.astype(f32)
        p1 = rest.astype(bf16)
        p2 = (rest - p1.astype(f32)).astype(bf16)
        total = dot(tri, p0) + (dot(tri, p1) + dot(tri, p2))
        cum[layer] = total
        cumt[layer] = jnp.transpose(total)
        b = sigmoid(x)
        beta[layer] = b
        betat[layer] = jnp.transpose(b)

    def conv(x, slot, taps):
        xs[slot] = x.astype(f32)
        total = xs[slot, RIM : RIM + T, :] * taps[CONV - 1 : CONV]
        for j in range(CONV - 1):
            total = total + xs[slot, RIM - 3 + j : RIM - 3 + j + T, :] * keep[j] * taps[j : j + 1]
        return total * sigmoid(total)

    def unit(x):
        return x * lax.rsqrt(jnp.sum(x * x, axis=-1, keepdims=True) + 1e-6)

    def prep(step, carry):
        layer = step // NK
        j = step % NK
        here = pl.ds(pl.multiple_of(j * D, D), D)
        key_at = pl.ds(pl.multiple_of(s * HQ + j * D, D), D)
        kcol = pl.ds(pl.multiple_of(2 * HQ + s * HQ + j * D, D), D)
        kn = unit(conv(kbuf[layer, :, here], 0, small[layer, 0:8, kcol]))
        qn = unit(conv(qbuf[layer, :, here], 1, small[layer, 0:8, key_at]))
        ks, qs = split(kn), split(qn)
        gram = mm(ks, ks, dot_nt)
        qk = mm(qs, ks, dot_nt)
        knt = jnp.transpose(kn)
        parts, held = [], []
        for u in range(REP):
            h = j * REP + u
            hh = s * NH + h
            cc = jnp.sum(jnp.where(lane == hh, cum[layer], 0.0), axis=1, keepdims=True)
            bc = jnp.sum(jnp.where(lane == hh + 2 * NH, beta[layer], 0.0), axis=1, keepdims=True)
            cr = cumt[layer, pl.ds(hh, 1), :]
            br = betat[layer, pl.ds(hh + 2 * NH, 1), :]
            decay = jnp.where(pair[...] > 0.0, jnp.exp(cc - cr), 0.0)
            low = jnp.where(trow > tcol, bc * gram * decay, 0.0)
            fs = jnp.exp(cc) * keep[CONV - 1]
            held.append((h, br, decay, fs, low))
            for i in range(T // D):
                parts.append(low[i * D : (i + 1) * D, i * D : (i + 1) * D])
        inv = inverses(parts, [dmask[i] for i in range(len(SIZES))])
        for u in range(REP):
            h, br, decay, fs, low = held[u]
            t1, t2 = inv[2 * u], inv[2 * u + 1]
            t21 = -mm(split(mm(split(t2), split(low[D:, :D]))), split(t1))
            top = jnp.concatenate([t1, jnp.zeros((D, D), f32)], axis=1)
            bottom = jnp.concatenate([t21, t2], axis=1)
            r = split(jnp.concatenate([top, bottom], axis=0) * br)
            z = split(
                mm(split(jnp.concatenate([decay * qk, knt * decay[T - 1 : T, :]], axis=0)), r)
            )
            eye = jnp.where(row == col, fs[T - 1 : T, :], 0.0)
            y = jnp.concatenate([fs * qn, eye], axis=0) - mm(z, split(fs * kn))
            zh[layer, h], zl[layer, h] = z
            yh[layer, h], yl[layer, h] = split(y)
        return carry

    lax.fori_loop(0, 2 * NK, prep, 0)

    out_copies = []
    for layer in range(2):
        src = vbuf.at[1, body] if layer == 0 else o1
        chain = [
            remote(
                s_out.at[layer, h], s_in.at[layer, h],
                c_send.at[layer, h], c_recv.at[layer, h], ahead,
            )
            for h in range(NH)
        ]
        if layer == 1:

            @pl.when(has_prev)
            def _():
                rim1.wait_recv()

        for h in range(NH):
            tcols = pl.ds(pl.multiple_of(4 * HQ + s * HV + h * D, D), D)
            v = split(conv(vbuf[layer, :, h * D : (h + 1) * D], h, small[layer, 0:8, tcols]))
            bv[h] = mm((zh[layer, h], zl[layer, h]), v)
        for h in range(NH):

            @pl.when(has_prev)
            def _():
                chain[h].wait_recv()

            start = split(s_in[layer, h])
            s_out[layer, h] = bv[h, T:, :] + mm((yh[layer, h, T:, :], yl[layer, h, T:, :]), start)

            @pl.when(has_next)
            def _():
                chain[h].start()

        gain = small[layer, 4:5, 0:D]
        for h in range(NH):
            start = split(s_in[layer, h])
            mixed = bv[h, :T, :] + mm((yh[layer, h, :T, :], yl[layer, h, :T, :]), start)
            scale = lax.rsqrt(jnp.mean(mixed * mixed, axis=-1, keepdims=True) + 1e-6)
            g = gbuf[layer, :, h * D : (h + 1) * D].astype(f32)
            value = (mixed * scale * gain * (g * sigmoid(g))).astype(bf16)
            if layer == 0:
                vbuf[1, RIM:, h * D : (h + 1) * D] = value
            else:
                o1[:, h * D : (h + 1) * D] = value
        if layer == 0:
            rim1 = remote(vbuf.at[1, pl.ds(T, RIM)], vbuf.at[1, rim], v_send, v_recv, ahead)

            @pl.when(has_next)
            def _():
                rim1.start()

        across = remote(src, out.at[0, :, cols(s, HV)], o_send, o_recv, partner)
        along = pltpu.make_async_copy(src, out.at[0, :, cols(s, HV)], o_loc)
        out_copies.append((chain, across, along))

        @pl.when(s == layer)
        def _():
            along.start()

        @pl.when(s != layer)
        def _():
            across.start()

    across, along = out_copies[1][1:]
    across.wait_recv()
    across.wait_send()
    along.wait()

    @pl.when(has_next)
    def _():
        for cp in rims:
            cp.wait_send()
        rim1.wait_send()
        for chain, _, _ in out_copies:
            for cp in chain:
                cp.wait_send()

    for cp in swaps:
        cp.wait_send()


def local(
    nctx, queries_in, keys_in, values_in, gate_in, decay_in, write_in, decay_log,
    conv_query, conv_key, conv_value, norm_gain, segment_ids,
):
    T = segment_ids.shape[0]
    heads = decay_in.shape[2]
    hq = queries_in.shape[2] // 2
    hv = values_in.shape[1] // 2
    nh = heads // 2
    dw = jnp.concatenate(
        [decay_in[0], write_in[0], jnp.zeros((T, D - 2 * heads), f32)], axis=1
    )
    taps = jnp.concatenate([conv_query[0], conv_key[0], conv_value[0]], axis=1).astype(f32)
    width = taps.shape[1]
    small = jnp.concatenate(
        [
            taps,
            jnp.pad(norm_gain, ((0, 0), (0, width - norm_gain.shape[1]))),
            jnp.pad(decay_log, ((0, 0), (0, width - heads))),
            jnp.zeros((2, width), f32),
        ],
        axis=0,
    )
    seg = jnp.broadcast_to(segment_ids[None], (8, T))
    dma = pltpu.SemaphoreType.DMA
    V = pltpu.VMEM
    return pl.pallas_call(
        functools.partial(kernel, nctx),
        out_shape=jax.ShapeDtypeStruct((1, T, 2 * hv), bf16),
        in_specs=[pl.BlockSpec(memory_space=pl.ANY)] * 7,
        out_specs=pl.BlockSpec(memory_space=pl.ANY),
        scratch_shapes=[
            V((2, RIM + T, hq), bf16),
            V((2, RIM + T, hq), bf16),
            V((2, RIM + T, hv), bf16),
            V((2, T, hv), bf16),
            V((2, T, D), f32),
            V((2, 8, width), f32),
            V((8, T), jnp.int32),
            V((8, T), jnp.int32),
            V((T, hv), bf16),
            V((nh, RIM + T, D), f32),
            V((RIM + T, D), f32),
            V((CONV, T, D), f32),
            V((T, T), f32),
            V((len(SIZES), D, D), f32),
            V((2, T, D), f32),
            V((2, D, T), f32),
            V((2, T, D), f32),
            V((2, D, T), f32),
            V((2, nh, T + D, T), bf16),
            V((2, nh, T + D, T), bf16),
            V((2, nh, T + D, D), bf16),
            V((2, nh, T + D, D), bf16),
            V((nh, T + D, D), f32),
            V((2, nh, D, D), f32),
            V((2, nh, D, D), f32),
            dma((7,)),
            dma((5,)),
            dma((5,)),
            dma((6,)),
            dma((6,)),
            dma((2, nh)),
            dma((2, nh)),
            dma,
            dma,
            dma,
            dma,
            dma,
        ],
        compiler_params=pltpu.CompilerParams(
            collective_id=0, has_side_effects=True, vmem_limit_bytes=48 * 2**20
        ),
        name="mixer",
    )(queries_in, keys_in, values_in, gate_in, dw, small, seg)


def solution(mesh):
    placed = (
        P("section", ("groups", "ctx"), "head"),
        P("section", ("groups", "ctx"), "head"),
        P(("groups", "ctx"), "head"),
        P("section", ("groups", "ctx"), "head"),
        P("section", ("groups", "ctx"), "head"),
        P("section", ("groups", "ctx"), "head"),
        P("section", "head"),
        P("section", None, "head"),
        P("section", None, "head"),
        P("section", None, "head"),
        P("section", None),
        P(("groups", "ctx")),
    )
    return jax.shard_map(
        functools.partial(local, mesh.shape["ctx"]),
        mesh=mesh,
        in_specs=placed,
        out_specs=P("section", ("groups", "ctx"), "head"),
        check_vma=False,
    )
```

```python
import functools

import jax
import jax.numpy as jnp
from jax import lax
from jax.experimental import pallas as pl
from jax.experimental.pallas import tpu as pltpu
from jax.sharding import PartitionSpec as P

D = 128
RIM = 16
CONV = 4
SIZES = (1, 2, 4, 8, 16, 32, 64)
bf16 = jnp.bfloat16
f32 = jnp.float32
MESH = pl.DeviceIdType.MESH


def split(x):
    high = x.astype(bf16)
    return high, (x - high.astype(f32)).astype(bf16)


def dot(a, b):
    return jnp.dot(a, b, preferred_element_type=f32)


def dot_nt(a, b):
    return lax.dot_general(a, b, (((1,), (1,)), ((), ())), preferred_element_type=f32)


def mm(a, b):
    if a[0].shape[1] > D:
        return dot(a[0], b[0]) + (dot(a[0], b[1]) + dot(a[1], b[0]))
    both = jnp.concatenate(a, axis=1), jnp.concatenate([b[0], b[0]], axis=0)
    return dot(*both) + dot(a[0], b[1])


def mm_nt(a, b):
    both = jnp.concatenate(a, axis=1), jnp.concatenate([b[0], b[0]], axis=1)
    return dot_nt(*both) + dot_nt(a[0], b[1])


def sigmoid(x):
    return 1.0 / (1.0 + jnp.exp(-x))


def iota(shape, dim):
    return lax.broadcasted_iota(jnp.int32, shape, dim)


def inverses(parts, mask):
    eye = (iota((D, D), 0) == iota((D, D), 1)).astype(f32)
    inv = [eye - a * mask[0].astype(f32) for a in parts]
    parts = [split(a) for a in parts]
    for i in range(1, len(SIZES)):
        halves = [split(t) for t in inv]
        lower = [(a[0] * mask[i], a[1] * mask[i]) for a in parts]
        mid = [split(mm(t, a)) for t, a in zip(halves, lower)]
        inv = [t - mm(m, h) for t, m, h in zip(inv, mid, halves)]
    return inv


def kernel(
    nctx, q_in, k_in, v_in, g_in, d_in, w_in, log_in, cq_in, ck_in, cv_in, gain_in, seg_in, out,
    qbuf, kbuf, vbuf, gbuf, dw, small, seg, segp, o1,
    xs, segx, keep, pair, dmask, cum, cumt, beta, betat,
    zh, zl, yh, yl, bv, s_in, s_out,
    loc_sem, x_send, x_recv, r_send, r_recv, c_send, c_recv, o_send, o_recv, o_loc, v_send, v_recv,
):
    T = q_in.shape[1]
    HQ = q_in.shape[2] // 2
    HV = v_in.shape[1] // 2
    NH = HV // D
    NK = HQ // D
    REP = NH // NK
    s = lax.axis_index("section")
    o = 1 - s
    c = lax.axis_index("ctx")
    has_prev = c > 0
    has_next = c < nctx - 1

    def cols(half, width):
        return pl.ds(pl.multiple_of(half * width, width), width)

    body = pl.ds(RIM, T)
    tail = pl.ds(T - RIM, RIM)
    rim = pl.ds(0, RIM)

    local = [
        (q_in.at[0, :, cols(s, HQ)], qbuf.at[s, body]),
        (k_in.at[0, :, cols(s, HQ)], kbuf.at[s, body]),
        (g_in.at[0, :, cols(s, HV)], gbuf.at[s]),
        (v_in.at[:, cols(s, HV)], vbuf.at[0, body]),
        (d_in.at[0], dw.at[s, 0]),
        (w_in.at[0], dw.at[s, 1]),
    ]
    local = [pltpu.make_async_copy(a, b, loc_sem.at[i]) for i, (a, b) in enumerate(local)]
    for cp in local:
        cp.start()

    taps = (cq_in, ck_in, cv_in)
    small[s, 0:CONV, :] = jnp.concatenate([t[0].astype(f32) for t in taps], axis=1)
    small[s, CONV : CONV + 1, 0:D] = gain_in[...]
    small[s, CONV + 1 : CONV + 2, 0:D] = jnp.broadcast_to(
        jnp.concatenate([log_in[...], jnp.zeros((1, D - 2 * NH), f32)], axis=1), (1, D)
    )
    seg[...] = jnp.broadcast_to(seg_in[...], (8, T))

    barrier = pltpu.get_barrier_semaphore()
    pl.semaphore_signal(barrier, inc=1, device_id={"section": o}, device_id_type=MESH)
    for ok, other in ((has_prev, c - 1), (has_next, c + 1)):

        @pl.when(ok)
        def _():
            for sec in (s, o):
                pl.semaphore_signal(
                    barrier, inc=1, device_id={"ctx": other, "section": sec}, device_id_type=MESH
                )

    pl.semaphore_wait(
        barrier, 1 + 2 * has_prev.astype(jnp.int32) + 2 * has_next.astype(jnp.int32)
    )

    def remote(src, dst, send, recv, where):
        return pltpu.make_async_remote_copy(
            src_ref=src, dst_ref=dst, send_sem=send, recv_sem=recv,
            device_id=where, device_id_type=MESH,
        )

    partner = {"section": o}
    ahead = {"ctx": c + 1}
    ahead_o = {"ctx": c + 1, "section": o}
    swaps = [
        (d_in.at[0], dw.at[s, 0]),
        (w_in.at[0], dw.at[s, 1]),
        (small.at[s], small.at[s]),
        (k_in.at[0, :, cols(o, HQ)], kbuf.at[s, body]),
        (q_in.at[0, :, cols(o, HQ)], qbuf.at[s, body]),
        (g_in.at[0, :, cols(o, HV)], gbuf.at[s]),
    ]
    swaps = [
        remote(a, b, x_send.at[i], x_recv.at[i], partner) for i, (a, b) in enumerate(swaps)
    ]
    rims = [
        (seg, segp, ahead),
        (k_in.at[0, tail, cols(s, HQ)], kbuf.at[s, rim], ahead),
        (q_in.at[0, tail, cols(s, HQ)], qbuf.at[s, rim], ahead),
        (k_in.at[0, tail, cols(o, HQ)], kbuf.at[s, rim], ahead_o),
        (q_in.at[0, tail, cols(o, HQ)], qbuf.at[s, rim], ahead_o),
        (v_in.at[tail, cols(s, HV)], vbuf.at[0, rim], ahead),
    ]
    rims = [
        remote(a, b, r_send.at[i], r_recv.at[i], w) for i, (a, b, w) in enumerate(rims)
    ]

    @pl.when(has_next)
    def _():
        for cp in rims:
            cp.start()

    for cp in swaps:
        cp.start()

    @pl.when(jnp.logical_not(has_prev))
    def _():
        segp[...] = jnp.zeros_like(segp)
        for layer in range(2):
            kbuf[layer, 0:RIM, :] = jnp.zeros((RIM, HQ), bf16)
            qbuf[layer, 0:RIM, :] = jnp.zeros((RIM, HQ), bf16)
            vbuf[layer, 0:RIM, :] = jnp.zeros((RIM, HV), bf16)
            for h in range(NH):
                s_in[layer, h] = jnp.zeros((D, D), f32)

    row = iota((D, D), 0)
    col = iota((D, D), 1)
    for i, size in enumerate(SIZES):
        down = row // size
        right = col // size
        dmask[i] = jnp.where((down == right + 1) & (down % 2 == 1), 1.0, 0.0).astype(bf16)
    trow = iota((T, T), 0)
    tcol = iota((T, T), 1)

    for cp in local:
        cp.wait()
    for cp in swaps:
        cp.wait_recv()

    @pl.when(has_prev)
    def _():
        for cp in rims:
            cp.wait_recv()

    seg_row = seg[0:1, :].astype(f32)
    before = jnp.transpose(jnp.broadcast_to(segp[0:1, :].astype(f32), (D, T)))
    own = jnp.transpose(jnp.broadcast_to(seg_row, (D, T)))
    segx[0:RIM, :] = before[T - RIM :, :]
    segx[RIM:, :] = own
    for j in range(CONV - 1):
        keep[j] = jnp.where(segx[RIM - 3 + j : RIM - 3 + j + T, :] == own, 1.0, 0.0)
    last = before[T - 1 : T, :]
    keep[CONV - 1] = jnp.where(own == last, 1.0, 0.0)
    own_wide = jnp.concatenate([own] * (T // D), axis=1)
    pair[...] = jnp.where((own_wide == seg_row) & (trow >= tcol), 1.0, 0.0)

    lane = iota((T, D), 1)
    upper = jnp.where(trow <= tcol, 1.0, 0.0).astype(bf16)
    fill = jnp.zeros((D - 2 * NH, T), f32)
    for layer in range(2):
        x = dw[layer, 0]
        rate = jnp.broadcast_to(small[layer, CONV + 1 : CONV + 2, 0:D], (D, D))
        rate = jnp.transpose(rate)[0 : 2 * NH, 0:1]
        soft = jnp.maximum(x, 0.0) + jnp.log1p(jnp.exp(-jnp.abs(x)))
        decay = jnp.maximum(-jnp.exp(rate) * soft, -104.0)
        p0 = decay.astype(bf16).astype(f32)
        rest = decay - p0
        p1 = rest.astype(bf16).astype(f32)
        three = jnp.concatenate([p0, p1, rest - p1, jnp.zeros_like(x)], axis=0).astype(bf16)
        total = dot(three, upper)
        n = 2 * NH
        total = total[0:n] + (total[n : 2 * n] + total[2 * n : 3 * n])
        cumt[layer] = total
        cum[layer] = jnp.transpose(jnp.concatenate([total, fill], axis=0))
        b = sigmoid(dw[layer, 1])
        betat[layer] = b
        beta[layer] = jnp.transpose(jnp.concatenate([b, fill], axis=0))

    def conv(x, slot, taps):
        xs[slot] = x.astype(f32)
        total = xs[slot, RIM : RIM + T, :] * taps[CONV - 1 : CONV]
        for j in range(CONV - 1):
            total = total + xs[slot, RIM - 3 + j : RIM - 3 + j + T, :] * keep[j] * taps[j : j + 1]
        return total * sigmoid(total)

    def unit(x):
        return x * lax.rsqrt(jnp.sum(x * x, axis=-1, keepdims=True) + 1e-6)

    def prep(step, carry):
        layer = step // NK
        j = step % NK
        here = pl.ds(pl.multiple_of(j * D, D), D)
        key_at = pl.ds(pl.multiple_of(s * HQ + j * D, D), D)
        kcol = pl.ds(pl.multiple_of(2 * HQ + s * HQ + j * D, D), D)
        kn = unit(conv(kbuf[layer, :, here], 0, small[layer, 0:8, kcol]))
        qn = unit(conv(qbuf[layer, :, here], 1, small[layer, 0:8, key_at]))
        ks, qs = split(kn), split(qn)
        gram = mm_nt(ks, ks)
        qk = mm_nt(qs, ks)
        knt = jnp.transpose(kn)
        parts, held = [], []
        for u in range(REP):
            h = j * REP + u
            hh = s * NH + h
            cc = jnp.sum(jnp.where(lane == hh, cum[layer], 0.0), axis=1, keepdims=True)
            bc = jnp.sum(jnp.where(lane == hh, beta[layer], 0.0), axis=1, keepdims=True)
            cr = cumt[layer, pl.ds(hh, 1), :]
            br = betat[layer, pl.ds(hh, 1), :]
            decay = jnp.where(pair[...] > 0.0, jnp.exp(cc - cr), 0.0)
            low = jnp.where(trow > tcol, bc * gram * decay, 0.0)
            fs = jnp.exp(cc) * keep[CONV - 1]
            held.append((h, br, decay, fs, low))
            for i in range(T // D):
                parts.append(low[i * D : (i + 1) * D, i * D : (i + 1) * D])
        inv = inverses(parts, [dmask[i] for i in range(len(SIZES))])
        for u in range(REP):
            h, br, decay, fs, low = held[u]
            t1, t2 = inv[2 * u], inv[2 * u + 1]
            t21 = -mm(split(mm(split(t2), split(low[D:, :D]))), split(t1))
            top = jnp.concatenate([t1, jnp.zeros((D, D), f32)], axis=1)
            bottom = jnp.concatenate([t21, t2], axis=1)
            r = split(jnp.concatenate([top, bottom], axis=0) * br)
            z = split(
                mm(split(jnp.concatenate([decay * qk, knt * decay[T - 1 : T, :]], axis=0)), r)
            )
            eye = jnp.where(row == col, fs[T - 1 : T, :], 0.0)
            y = jnp.concatenate([fs * qn, eye], axis=0) - mm(z, split(fs * kn))
            zh[layer, h], zl[layer, h] = z
            yh[layer, h], yl[layer, h] = split(y)
        return carry

    chains = [
        [
            remote(
                s_out.at[layer, h], s_in.at[layer, h],
                c_send.at[layer, h], c_recv.at[layer, h], ahead,
            )
            for h in range(NH)
        ]
        for layer in range(2)
    ]
    rim1 = remote(vbuf.at[1, pl.ds(T, RIM)], vbuf.at[1, rim], v_send, v_recv, ahead)

    def increments(layer):
        for h in range(NH):
            tcols = pl.ds(pl.multiple_of(4 * HQ + s * HV + h * D, D), D)
            v = split(conv(vbuf[layer, :, h * D : (h + 1) * D], h, small[layer, 0:8, tcols]))
            bv[h] = mm((zh[layer, h], zl[layer, h]), v)

    def pass_on(layer):
        for h in range(NH):

            @pl.when(has_prev)
            def _():
                chains[layer][h].wait_recv()

            start = split(s_in[layer, h])
            s_out[layer, h] = bv[h, T:, :] + mm((yh[layer, h, T:, :], yl[layer, h, T:, :]), start)

            @pl.when(has_next)
            def _():
                chains[layer][h].start()

    def finish(layer):
        gain = small[layer, 4:5, 0:D]
        for h in range(NH):
            start = split(s_in[layer, h])
            mixed = bv[h, :T, :] + mm((yh[layer, h, :T, :], yl[layer, h, :T, :]), start)
            scale = lax.rsqrt(jnp.mean(mixed * mixed, axis=-1, keepdims=True) + 1e-6)
            g = gbuf[layer, :, h * D : (h + 1) * D].astype(f32)
            value = (mixed * scale * gain * (g * sigmoid(g))).astype(bf16)
            if layer == 0:
                vbuf[1, RIM:, h * D : (h + 1) * D] = value
            else:
                o1[:, h * D : (h + 1) * D] = value
        if layer == 0:

            @pl.when(has_next)
            def _():
                rim1.start()

        src = vbuf.at[1, body] if layer == 0 else o1
        across = remote(src, out.at[0, :, cols(s, HV)], o_send, o_recv, partner)
        along = pltpu.make_async_copy(src, out.at[0, :, cols(s, HV)], o_loc)

        @pl.when(s == layer)
        def _():
            along.start()

        @pl.when(s != layer)
        def _():
            across.start()

        return across, along

    lax.fori_loop(0, NK, prep, 0)
    increments(0)

    @pl.when(c <= 1)
    def _():
        pass_on(0)

    lax.fori_loop(NK, NK + NK // 2, prep, 0)

    @pl.when(c == 2)
    def _():
        pass_on(0)

    lax.fori_loop(NK + NK // 2, 2 * NK, prep, 0)

    @pl.when(c > 2)
    def _():
        pass_on(0)

    finish(0)

    @pl.when(has_prev)
    def _():
        rim1.wait_recv()

    increments(1)
    pass_on(1)
    across, along = finish(1)
    across.wait_recv()
    across.wait_send()
    along.wait()

    @pl.when(has_next)
    def _():
        for cp in rims:
            cp.wait_send()
        rim1.wait_send()
        for chain in chains:
            for cp in chain:
                cp.wait_send()

    for cp in swaps:
        cp.wait_send()


def local(
    nctx, queries_in, keys_in, values_in, gate_in, decay_in, write_in, decay_log,
    conv_query, conv_key, conv_value, norm_gain, segment_ids,
):
    T = segment_ids.shape[0]
    hq = queries_in.shape[2] // 2
    hv = values_in.shape[1] // 2
    nh = hv // D
    width = 4 * hq + 2 * hv
    dma = pltpu.SemaphoreType.DMA
    V = pltpu.VMEM
    return pl.pallas_call(
        functools.partial(kernel, nctx),
        out_shape=jax.ShapeDtypeStruct((1, T, 2 * hv), bf16),
        in_specs=[pl.BlockSpec(memory_space=pl.ANY)] * 6
        + [pl.BlockSpec(memory_space=pltpu.VMEM)] * 6,
        out_specs=pl.BlockSpec(memory_space=pl.ANY),
        scratch_shapes=[
            V((2, RIM + T, hq), bf16),
            V((2, RIM + T, hq), bf16),
            V((2, RIM + T, hv), bf16),
            V((2, T, hv), bf16),
            V((2, 2, 2 * nh, T), f32),
            V((2, 8, width), f32),
            V((8, T), jnp.int32),
            V((8, T), jnp.int32),
            V((T, hv), bf16),
            V((nh, RIM + T, D), f32),
            V((RIM + T, D), f32),
            V((CONV, T, D), f32),
            V((T, T), f32),
            V((len(SIZES), D, D), bf16),
            V((2, T, D), f32),
            V((2, 2 * nh, T), f32),
            V((2, T, D), f32),
            V((2, 2 * nh, T), f32),
            V((2, nh, T + D, T), bf16),
            V((2, nh, T + D, T), bf16),
            V((2, nh, T + D, D), bf16),
            V((2, nh, T + D, D), bf16),
            V((nh, T + D, D), f32),
            V((2, nh, D, D), f32),
            V((2, nh, D, D), f32),
            dma((6,)),
            dma((6,)),
            dma((6,)),
            dma((6,)),
            dma((6,)),
            dma((2, nh)),
            dma((2, nh)),
            dma,
            dma,
            dma,
            dma,
            dma,
        ],
        compiler_params=pltpu.CompilerParams(
            collective_id=0, has_side_effects=True, vmem_limit_bytes=60 * 2**20
        ),
        name="mixer",
    )(
        queries_in, keys_in, values_in, gate_in,
        jnp.swapaxes(decay_in, 1, 2), jnp.swapaxes(write_in, 1, 2),
        decay_log, conv_query, conv_key, conv_value, norm_gain, segment_ids.reshape(1, T),
    )


def solution(mesh):
    placed = (
        P("section", ("groups", "ctx"), "head"),
        P("section", ("groups", "ctx"), "head"),
        P(("groups", "ctx"), "head"),
        P("section", ("groups", "ctx"), "head"),
        P("section", ("groups", "ctx"), "head"),
        P("section", ("groups", "ctx"), "head"),
        P("section", "head"),
        P("section", None, "head"),
        P("section", None, "head"),
        P("section", None, "head"),
        P("section", None),
        P(("groups", "ctx")),
    )
    return jax.shard_map(
        functools.partial(local, mesh.shape["ctx"]),
        mesh=mesh,
        in_specs=placed,
        out_specs=P("section", ("groups", "ctx"), "head"),
        check_vma=False,
    )
```

```python
import functools

import jax
import jax.numpy as jnp
from jax import lax
from jax.experimental import pallas as pl
from jax.experimental.pallas import tpu as pltpu
from jax.sharding import PartitionSpec as P

D = 128
RIM = 16
CONV = 4
SIZES = (1, 2, 4, 8, 16, 32, 64)
bf16 = jnp.bfloat16
f32 = jnp.float32
MESH = pl.DeviceIdType.MESH


def split(x):
    high = x.astype(bf16)
    return high, (x - high.astype(f32)).astype(bf16)


def dot(a, b):
    return jnp.dot(a, b, preferred_element_type=f32)


def dot_nt(a, b):
    return lax.dot_general(a, b, (((1,), (1,)), ((), ())), preferred_element_type=f32)


def mm(a, b):
    if a[0].shape[1] > D:
        return dot(a[0], b[0]) + (dot(a[0], b[1]) + dot(a[1], b[0]))
    both = jnp.concatenate(a, axis=1), jnp.concatenate([b[0], b[0]], axis=0)
    return dot(*both) + dot(a[0], b[1])


def mm_nt(a, b):
    both = jnp.concatenate(a, axis=1), jnp.concatenate([b[0], b[0]], axis=1)
    return dot_nt(*both) + dot_nt(a[0], b[1])


def sigmoid(x):
    return 1.0 / (1.0 + jnp.exp(-x))


def iota(shape, dim):
    return lax.broadcasted_iota(jnp.int32, shape, dim)


def inverses(parts, mask):
    eye = (iota((D, D), 0) == iota((D, D), 1)).astype(f32)
    inv = [eye - a * mask[0].astype(f32) for a in parts]
    parts = [split(a) for a in parts]
    for i in range(1, len(SIZES)):
        halves = [split(t) for t in inv]
        lower = [(a[0] * mask[i], a[1] * mask[i]) for a in parts]
        mid = [split(mm(t, a)) for t, a in zip(halves, lower)]
        inv = [t - mm(m, h) for t, m, h in zip(inv, mid, halves)]
    return inv


def kernel(
    nctx, q_in, k_in, v_in, g_in, d_in, w_in, log_in, cq_in, ck_in, cv_in, gain_in, seg_in, out,
    qbuf, kbuf, vbuf, gbuf, dw, small, seg, segp, o1,
    xs, segx, keep, pair, dmask, cum, cumt, beta, betat,
    zh, zl, yh, yl, bv, s_in, s_out,
    loc_sem, x_send, x_recv, r_send, r_recv, c_send, c_recv, o_send, o_recv, o_loc, v_send, v_recv,
):
    T = q_in.shape[1]
    HQ = q_in.shape[2] // 2
    HV = v_in.shape[1] // 2
    NH = HV // D
    NK = HQ // D
    REP = NH // NK
    s = lax.axis_index("section")
    o = 1 - s
    c = lax.axis_index("ctx")
    has_prev = c > 0
    has_next = c < nctx - 1

    def cols(half, width):
        return pl.ds(pl.multiple_of(half * width, width), width)

    body = pl.ds(RIM, T)
    tail = pl.ds(T - RIM, RIM)
    rim = pl.ds(0, RIM)

    local = [
        (q_in.at[0, :, cols(s, HQ)], qbuf.at[s, body]),
        (k_in.at[0, :, cols(s, HQ)], kbuf.at[s, body]),
        (g_in.at[0, :, cols(s, HV)], gbuf.at[s]),
        (v_in.at[:, cols(s, HV)], vbuf.at[0, body]),
        (d_in.at[0], dw.at[s, 0]),
        (w_in.at[0], dw.at[s, 1]),
    ]
    local = [pltpu.make_async_copy(a, b, loc_sem.at[i]) for i, (a, b) in enumerate(local)]
    for cp in local:
        cp.start()

    taps = (cq_in, ck_in, cv_in)
    small[s, 0:CONV, :] = jnp.concatenate([t[0].astype(f32) for t in taps], axis=1)
    small[s, CONV : CONV + 1, 0:D] = gain_in[...]
    small[s, CONV + 1 : CONV + 2, 0:D] = jnp.broadcast_to(
        jnp.concatenate([log_in[...], jnp.zeros((1, D - 2 * NH), f32)], axis=1), (1, D)
    )
    seg[...] = jnp.broadcast_to(seg_in[...], (8, T))

    barrier = pltpu.get_barrier_semaphore()
    pl.semaphore_signal(barrier, inc=1, device_id={"section": o}, device_id_type=MESH)
    for ok, other in ((has_prev, c - 1), (has_next, c + 1)):

        @pl.when(ok)
        def _():
            for sec in (s, o):
                pl.semaphore_signal(
                    barrier, inc=1, device_id={"ctx": other, "section": sec}, device_id_type=MESH
                )

    pl.semaphore_wait(
        barrier, 1 + 2 * has_prev.astype(jnp.int32) + 2 * has_next.astype(jnp.int32)
    )

    def remote(src, dst, send, recv, where):
        return pltpu.make_async_remote_copy(
            src_ref=src, dst_ref=dst, send_sem=send, recv_sem=recv,
            device_id=where, device_id_type=MESH,
        )

    partner = {"section": o}
    ahead = {"ctx": c + 1}
    ahead_o = {"ctx": c + 1, "section": o}
    swaps = [
        (d_in.at[0], dw.at[s, 0]),
        (w_in.at[0], dw.at[s, 1]),
        (small.at[s], small.at[s]),
        (k_in.at[0, :, cols(o, HQ)], kbuf.at[s, body]),
        (q_in.at[0, :, cols(o, HQ)], qbuf.at[s, body]),
        (g_in.at[0, :, cols(o, HV)], gbuf.at[s]),
    ]
    swaps = [
        remote(a, b, x_send.at[i], x_recv.at[i], partner) for i, (a, b) in enumerate(swaps)
    ]
    rims = [
        (seg, segp, ahead),
        (k_in.at[0, tail, cols(s, HQ)], kbuf.at[s, rim], ahead),
        (q_in.at[0, tail, cols(s, HQ)], qbuf.at[s, rim], ahead),
        (k_in.at[0, tail, cols(o, HQ)], kbuf.at[s, rim], ahead_o),
        (q_in.at[0, tail, cols(o, HQ)], qbuf.at[s, rim], ahead_o),
        (v_in.at[tail, cols(s, HV)], vbuf.at[0, rim], ahead),
    ]
    rims = [
        remote(a, b, r_send.at[i], r_recv.at[i], w) for i, (a, b, w) in enumerate(rims)
    ]

    @pl.when(has_next)
    def _():
        for cp in rims:
            cp.start()

    for cp in swaps:
        cp.start()

    @pl.when(jnp.logical_not(has_prev))
    def _():
        segp[...] = jnp.zeros_like(segp)
        for layer in range(2):
            kbuf[layer, 0:RIM, :] = jnp.zeros((RIM, HQ), bf16)
            qbuf[layer, 0:RIM, :] = jnp.zeros((RIM, HQ), bf16)
            vbuf[layer, 0:RIM, :] = jnp.zeros((RIM, HV), bf16)
            for h in range(NH):
                s_in[layer, h] = jnp.zeros((D, D), f32)

    row = iota((D, D), 0)
    col = iota((D, D), 1)
    for i, size in enumerate(SIZES):
        down = row // size
        right = col // size
        dmask[i] = jnp.where((down == right + 1) & (down % 2 == 1), 1.0, 0.0).astype(bf16)
    trow = iota((T, T), 0)
    tcol = iota((T, T), 1)

    for cp in local:
        cp.wait()
    for cp in swaps:
        cp.wait_recv()

    @pl.when(has_prev)
    def _():
        for cp in rims:
            cp.wait_recv()

    seg_row = seg[0:1, :].astype(f32)
    before = jnp.transpose(jnp.broadcast_to(segp[0:1, :].astype(f32), (D, T)))
    own = jnp.transpose(jnp.broadcast_to(seg_row, (D, T)))
    segx[0:RIM, :] = before[T - RIM :, :]
    segx[RIM:, :] = own
    for j in range(CONV - 1):
        keep[j] = jnp.where(segx[RIM - 3 + j : RIM - 3 + j + T, :] == own, 1.0, 0.0)
    last = before[T - 1 : T, :]
    keep[CONV - 1] = jnp.where(own == last, 1.0, 0.0)
    own_wide = jnp.concatenate([own] * (T // D), axis=1)
    pair[...] = jnp.where((own_wide == seg_row) & (trow >= tcol), 1.0, 0.0)

    lane = iota((T, D), 1)
    upper = jnp.where(trow <= tcol, 1.0, 0.0).astype(bf16)
    fill = jnp.zeros((D - 2 * NH, T), f32)
    for layer in range(2):
        x = dw[layer, 0]
        rate = jnp.broadcast_to(small[layer, CONV + 1 : CONV + 2, 0:D], (D, D))
        rate = jnp.transpose(rate)[0 : 2 * NH, 0:1]
        soft = jnp.maximum(x, 0.0) + jnp.log1p(jnp.exp(-jnp.abs(x)))
        decay = jnp.maximum(-jnp.exp(rate) * soft, -104.0)
        p0 = decay.astype(bf16).astype(f32)
        rest = decay - p0
        p1 = rest.astype(bf16).astype(f32)
        three = jnp.concatenate([p0, p1, rest - p1, jnp.zeros_like(x)], axis=0).astype(bf16)
        total = dot(three, upper)
        n = 2 * NH
        total = total[0:n] + (total[n : 2 * n] + total[2 * n : 3 * n])
        cumt[layer] = total
        cum[layer] = jnp.transpose(jnp.concatenate([total, fill], axis=0))
        b = sigmoid(dw[layer, 1])
        betat[layer] = b
        beta[layer] = jnp.transpose(jnp.concatenate([b, fill], axis=0))

    def conv(x, slot, taps):
        xs[slot] = x.astype(f32)
        total = xs[slot, RIM : RIM + T, :] * taps[CONV - 1 : CONV]
        for j in range(CONV - 1):
            total = total + xs[slot, RIM - 3 + j : RIM - 3 + j + T, :] * keep[j] * taps[j : j + 1]
        return total * sigmoid(total)

    def unit(x):
        return x * lax.rsqrt(jnp.sum(x * x, axis=-1, keepdims=True) + 1e-6)

    def prep(layer):
        parts, held, keyed = [], [], []
        for j in range(NK):
            here = pl.ds(j * D, D)
            key_at = pl.ds(pl.multiple_of(s * HQ + j * D, D), D)
            kcol = pl.ds(pl.multiple_of(2 * HQ + s * HQ + j * D, D), D)
            kn = unit(conv(kbuf[layer, :, here], 2 * j, small[layer, 0:8, kcol]))
            qn = unit(conv(qbuf[layer, :, here], 2 * j + 1, small[layer, 0:8, key_at]))
            ks, qs = split(kn), split(qn)
            gram = mm_nt(ks, ks)
            qk = mm_nt(qs, ks)
            keyed.append((kn, qn, qk, jnp.transpose(kn)))
            for u in range(REP):
                h = j * REP + u
                hh = s * NH + h
                cc = jnp.sum(jnp.where(lane == hh, cum[layer], 0.0), axis=1, keepdims=True)
                bc = jnp.sum(jnp.where(lane == hh, beta[layer], 0.0), axis=1, keepdims=True)
                cr = cumt[layer, pl.ds(hh, 1), :]
                br = betat[layer, pl.ds(hh, 1), :]
                decay = jnp.where(pair[...] > 0.0, jnp.exp(cc - cr), 0.0)
                low = jnp.where(trow > tcol, bc * gram * decay, 0.0)
                fs = jnp.exp(cc) * keep[CONV - 1]
                held.append((br, decay, fs, low[D:, :D]))
                for i in range(T // D):
                    parts.append(low[i * D : (i + 1) * D, i * D : (i + 1) * D])
        inv = inverses(parts, [dmask[i] for i in range(len(SIZES))])
        for h in range(NH):
            br, decay, fs, low = held[h]
            kn, qn, qk, knt = keyed[h // REP]
            t1, t2 = inv[2 * h], inv[2 * h + 1]
            t21 = -mm(split(mm(split(t2), split(low))), split(t1))
            top = jnp.concatenate([t1, jnp.zeros((D, D), f32)], axis=1)
            bottom = jnp.concatenate([t21, t2], axis=1)
            r = split(jnp.concatenate([top, bottom], axis=0) * br)
            z = split(
                mm(split(jnp.concatenate([decay * qk, knt * decay[T - 1 : T, :]], axis=0)), r)
            )
            eye = jnp.where(row == col, fs[T - 1 : T, :], 0.0)
            y = jnp.concatenate([fs * qn, eye], axis=0) - mm(z, split(fs * kn))
            zh[layer, h], zl[layer, h] = z
            yh[layer, h], yl[layer, h] = split(y)

    chains = [
        [
            remote(
                s_out.at[layer, h], s_in.at[layer, h],
                c_send.at[layer, h], c_recv.at[layer, h], ahead,
            )
            for h in range(NH)
        ]
        for layer in range(2)
    ]
    rim1 = remote(vbuf.at[1, pl.ds(T, RIM)], vbuf.at[1, rim], v_send, v_recv, ahead)

    def increments(layer):
        for h in range(NH):
            tcols = pl.ds(pl.multiple_of(4 * HQ + s * HV + h * D, D), D)
            v = split(conv(vbuf[layer, :, h * D : (h + 1) * D], h, small[layer, 0:8, tcols]))
            bv[h] = mm((zh[layer, h], zl[layer, h]), v)

    def pass_on(layer):
        for h in range(NH):

            @pl.when(has_prev)
            def _():
                chains[layer][h].wait_recv()

            start = split(s_in[layer, h])
            s_out[layer, h] = bv[h, T:, :] + mm((yh[layer, h, T:, :], yl[layer, h, T:, :]), start)

            @pl.when(has_next)
            def _():
                chains[layer][h].start()

    def finish(layer):
        gain = small[layer, 4:5, 0:D]
        for h in range(NH):
            start = split(s_in[layer, h])
            mixed = bv[h, :T, :] + mm((yh[layer, h, :T, :], yl[layer, h, :T, :]), start)
            scale = lax.rsqrt(jnp.mean(mixed * mixed, axis=-1, keepdims=True) + 1e-6)
            g = gbuf[layer, :, h * D : (h + 1) * D].astype(f32)
            value = (mixed * scale * gain * (g * sigmoid(g))).astype(bf16)
            if layer == 0:
                vbuf[1, RIM:, h * D : (h + 1) * D] = value
            else:
                o1[:, h * D : (h + 1) * D] = value
        if layer == 0:

            @pl.when(has_next)
            def _():
                rim1.start()

        src = vbuf.at[1, body] if layer == 0 else o1
        across = remote(src, out.at[0, :, cols(s, HV)], o_send, o_recv, partner)
        along = pltpu.make_async_copy(src, out.at[0, :, cols(s, HV)], o_loc)

        @pl.when(s == layer)
        def _():
            along.start()

        @pl.when(s != layer)
        def _():
            across.start()

        return across, along

    def turn(layer, carry):
        prep(layer)

        @pl.when(layer == 0)
        def _():
            increments(0)

            @pl.when(c <= 1)
            def _():
                pass_on(0)

        return carry

    lax.fori_loop(0, 2, turn, 0)

    @pl.when(c > 1)
    def _():
        pass_on(0)

    finish(0)

    @pl.when(has_prev)
    def _():
        rim1.wait_recv()

    increments(1)
    pass_on(1)
    across, along = finish(1)
    across.wait_recv()
    across.wait_send()
    along.wait()

    @pl.when(has_next)
    def _():
        for cp in rims:
            cp.wait_send()
        rim1.wait_send()
        for chain in chains:
            for cp in chain:
                cp.wait_send()

    for cp in swaps:
        cp.wait_send()


def local(
    nctx, queries_in, keys_in, values_in, gate_in, decay_in, write_in, decay_log,
    conv_query, conv_key, conv_value, norm_gain, segment_ids,
):
    T = segment_ids.shape[0]
    hq = queries_in.shape[2] // 2
    hv = values_in.shape[1] // 2
    nh = hv // D
    width = 4 * hq + 2 * hv
    dma = pltpu.SemaphoreType.DMA
    V = pltpu.VMEM
    return pl.pallas_call(
        functools.partial(kernel, nctx),
        out_shape=jax.ShapeDtypeStruct((1, T, 2 * hv), bf16),
        in_specs=[pl.BlockSpec(memory_space=pl.ANY)] * 6
        + [pl.BlockSpec(memory_space=pltpu.VMEM)] * 6,
        out_specs=pl.BlockSpec(memory_space=pl.ANY),
        scratch_shapes=[
            V((2, RIM + T, hq), bf16),
            V((2, RIM + T, hq), bf16),
            V((2, RIM + T, hv), bf16),
            V((2, T, hv), bf16),
            V((2, 2, 2 * nh, T), f32),
            V((2, 8, width), f32),
            V((8, T), jnp.int32),
            V((8, T), jnp.int32),
            V((T, hv), bf16),
            V((max(nh, 2 * (hq // D)), RIM + T, D), f32),
            V((RIM + T, D), f32),
            V((CONV, T, D), f32),
            V((T, T), f32),
            V((len(SIZES), D, D), bf16),
            V((2, T, D), f32),
            V((2, 2 * nh, T), f32),
            V((2, T, D), f32),
            V((2, 2 * nh, T), f32),
            V((2, nh, T + D, T), bf16),
            V((2, nh, T + D, T), bf16),
            V((2, nh, T + D, D), bf16),
            V((2, nh, T + D, D), bf16),
            V((nh, T + D, D), f32),
            V((2, nh, D, D), f32),
            V((2, nh, D, D), f32),
            dma((6,)),
            dma((6,)),
            dma((6,)),
            dma((6,)),
            dma((6,)),
            dma((2, nh)),
            dma((2, nh)),
            dma,
            dma,
            dma,
            dma,
            dma,
        ],
        compiler_params=pltpu.CompilerParams(
            collective_id=0, has_side_effects=True, vmem_limit_bytes=60 * 2**20
        ),
        name="mixer",
    )(
        queries_in, keys_in, values_in, gate_in,
        jnp.swapaxes(decay_in, 1, 2), jnp.swapaxes(write_in, 1, 2),
        decay_log, conv_query, conv_key, conv_value, norm_gain, segment_ids.reshape(1, T),
    )


def solution(mesh):
    placed = (
        P("section", ("groups", "ctx"), "head"),
        P("section", ("groups", "ctx"), "head"),
        P(("groups", "ctx"), "head"),
        P("section", ("groups", "ctx"), "head"),
        P("section", ("groups", "ctx"), "head"),
        P("section", ("groups", "ctx"), "head"),
        P("section", "head"),
        P("section", None, "head"),
        P("section", None, "head"),
        P("section", None, "head"),
        P("section", None),
        P(("groups", "ctx")),
    )
    return jax.shard_map(
        functools.partial(local, mesh.shape["ctx"]),
        mesh=mesh,
        in_specs=placed,
        out_specs=P("section", ("groups", "ctx"), "head"),
        check_vma=False,
    )
```
